32 devices in a mesh: gx: 8 (over y, x, core), gy: 4 (over z).
Axes of the slice: x: 2, y: 2, z: 4, core: 2. Of those that a mesh axis runs over, the one named last changes fastest.
Arguments:
- right_side: float32 [128, 512], P('gx', 'gy'), may hold values from -18 to 18
- class_map: int32 [128, 512], P('gx', 'gy'), may hold values from 0 to 15
- class_values: float32 [16], replicated, may hold values from 0.3 to 30
- kept_counts: int32 [8, 4], P('gx', 'gy'), may hold values from 10 to 20
- factors: bfloat16 [8, 4, 18, 256, 256], P('gx', 'gy'), may hold values from -2 to 2
- basis: bfloat16 [8, 4, 20, 32, 144], P('gx', 'gy'), may hold values from -0.09375 to 0.09375
- coarse_factor: bfloat16 [640, 640], P(('gx', 'gy')), may hold values from -0.4375 to 0.4375
Outputs:
- solution_field: float32 [128, 512], P('gx', 'gy')
- residual: float32 [128, 512], P('gx', 'gy')
- preconditioned: float32 [128, 512], P('gx', 'gy')
The draws below stay inside these ranges and needn't reach their ends.
Inputs may be any that keep to these rules, and one draw needn't show every extreme that they name: `kept_counts`: basis vectors of index 10 and above may be unused in a subdomain.
All inputs are finite; a program needn't handle non-finite values.
Results may differ from the reference program's by a relative error of at most 0.023.
Values may be sent and summed in bfloat16 or wider, within the bound.
A program may use at most 64 MiB of HBM per device.

```python
import math
import jax
import jax.numpy as jnp
from jax import lax

CX = 16
CY = 128
OV = 8
NEV = 20
BLOCK = 256
CLASSES = 16
ITERS = 3
SUBX = 8
SUBY = 4
NX = 128
NY = 512
EX = 32
EY = 144
NB = 18
K = 640


def draw_right_side(key, part):
    key = jax.random.fold_in(key, 5)
    first = jax.random.fold_in(key, 0)
    row_grid = lax.broadcasted_iota(jnp.int32, (NX, NY), 0).astype(jnp.float32)
    ramp = 1.0 + 2.0 * row_grid / NX
    values = jax.random.truncated_normal(first, -6.0, 6.0, (NX, NY), jnp.float32) * ramp
    return values.astype(jnp.float32)


def draw_factors(key, part):
    key = jax.random.fold_in(key, 11)
    first, second = jax.random.split(key, 2)
    shape = (SUBX, SUBY, NB, BLOCK, BLOCK)
    spread = jax.random.truncated_normal(first, -6.0, 6.0, shape, jnp.float32)
    diagonal = jnp.exp(jax.random.uniform(second, (SUBX, SUBY, NB, BLOCK, 1), jnp.float32, math.log(0.25), math.log(0.6)))
    row_grid = lax.broadcasted_iota(jnp.int32, (BLOCK, BLOCK), 0)
    column_grid = lax.broadcasted_iota(jnp.int32, (BLOCK, BLOCK), 1)
    identity = (row_grid == column_grid).astype(jnp.float32)
    values = 0.35 / math.sqrt(BLOCK) * spread + identity * diagonal
    return values.astype(jnp.bfloat16)


def place_ends(result, stream_key, smallest, top_value):
    longest = result.shape.index(max(result.shape))
    spots = []
    for shift in (0, 1):
        where = [jax.random.randint(jax.random.fold_in(stream_key, axis), (), 0, length) for axis, length in enumerate(result.shape)]
        where[longest] = (where[longest] + shift) % result.shape[longest]
        spots.append(tuple(where))
    return result.at[spots[0]].set(smallest).at[spots[1]].set(top_value)


def strengthened(result, stream_key, source, target, blocks, factor):
    owner, partner = [(jnp.arange(result.shape[dim]) // (result.shape[dim] // blocks)).reshape([-1 if axis == dim else 1 for axis in range(result.ndim)]) for dim in (source, target)]
    chosen = jax.random.permutation(stream_key, blocks)[partner]
    strong = (owner == chosen) | (owner == (partner + blocks // 2) % blocks)
    return jnp.where(strong, factor * result, result)


def block_scale(stream_key, dims, shards, low, high):
    def one(axis_at, parts):
        steps = jax.random.uniform(jax.random.fold_in(jax.random.fold_in(stream_key, 6), axis_at), (parts,), jnp.float32, low / len(shards), high / len(shards))
        return jnp.repeat(jnp.exp(steps), dims[axis_at] // parts).reshape((-1,) + (1,) * (len(dims) - axis_at - 1))

    level = one(*shards[0])
    for cut in shards[1:]:
        level = level * one(*cut)
    return level


def scatter_about(own_key, dims, scale, reach, shards=(), held_as=jnp.bfloat16):
    factor_of = block_scale(own_key, dims, shards, -0.22, 0.18) if shards else 1.0
    entries = jax.random.normal(own_key, dims, jnp.float32) * scale * factor_of
    return jnp.minimum(jnp.maximum(entries, -reach), reach).astype(held_as)


def bell_draw_with(own_key, shape, scale, most, pieces, heavy, kind=jnp.bfloat16):
    entries = scale * jax.random.normal(own_key, shape, jnp.float32)
    if pieces:
        entries = entries * block_scale(own_key, shape, pieces, -0.22, 0.18)
    return jnp.clip(strengthened(entries, jax.random.fold_in(own_key, 3), *heavy), -most, most).astype(kind)


def setup_inputs(seed: int = 0) -> dict:
    arg_keys = jax.random.split(jax.random.key(seed), 8)
    return {
        "right_side": draw_right_side(jax.random.fold_in(arg_keys[7], 71), 0),
        "class_map": place_ends(jax.random.randint(arg_keys[1], (NX, NY), 0, CLASSES), jax.random.fold_in(arg_keys[1], 1), 0, CLASSES - 1).astype(jnp.int32),
        "class_values": jnp.clip(jnp.exp(jax.random.uniform(arg_keys[2], (CLASSES,), jnp.float32, math.log(0.3), math.log(30.0))), 0.3, 30.0),
        "kept_counts": place_ends(jax.random.randint(arg_keys[3], (SUBX, SUBY), NEV // 2, NEV + 1), jax.random.fold_in(arg_keys[3], 1), NEV // 2, NEV).astype(jnp.int32),
        "factors": draw_factors(jax.random.fold_in(arg_keys[7], 71), 0),
        "basis": scatter_about(arg_keys[5], (SUBX, SUBY, NEV, EX, EY), (EX * EY) ** -0.5, 0.09375, ((0, 8), (1, 4))),
        "coarse_factor": bell_draw_with(arg_keys[6], (K, K), K ** -0.5, 0.4375, ((0, 32),), (0, 1, 32, 2.75)),
    }


def coefficients(conductivity):
    padded = jnp.pad(conductivity, 1)
    face_north = 0.5 * (conductivity + padded[:-2, 1:-1])
    face_south = 0.5 * (conductivity + padded[2:, 1:-1])
    face_west = 0.5 * (conductivity + padded[1:-1, :-2])
    face_east = 0.5 * (conductivity + padded[1:-1, 2:])
    return face_north, face_south, face_west, face_east


def operate(field, faces):
    padded = jnp.pad(field, 1)
    face_north, face_south, face_west, face_east = faces
    return (face_north * (field - padded[:-2, 1:-1]) + face_south * (field - padded[2:, 1:-1])
            + face_west * (field - padded[1:-1, :-2]) + face_east * (field - padded[1:-1, 2:]))


def precondition(residual, factors, basis, coarse_factor, keep):
    rounded = residual.astype(jnp.bfloat16)
    padded = jnp.pad(rounded, OV)
    ext_rows = CX + 2 * OV
    ext_columns = CY + 2 * OV
    count = SUBX * SUBY
    indices = jnp.arange(count, dtype=jnp.int32)

    def extended_box(index):
        row_index = (index // SUBY).astype(jnp.int32)
        column_index = (index % SUBY).astype(jnp.int32)
        box = lax.dynamic_slice(padded, (row_index * CX, column_index * CY), (ext_rows, ext_columns))
        return box, row_index, column_index

    def restrict(index):
        box, row_index, column_index = extended_box(index)
        vectors = basis[row_index, column_index].astype(jnp.float32)
        return jnp.einsum("kxy,xy->k", vectors, box.astype(jnp.float32))

    restricted = lax.map(restrict, indices).reshape(-1) * keep
    coarse_in = restricted.astype(jnp.bfloat16)
    coarse_mid = jnp.dot(coarse_factor, coarse_in, preferred_element_type=jnp.float32) * keep
    coarse_out = jnp.dot(coarse_mid.astype(jnp.bfloat16), coarse_factor, preferred_element_type=jnp.float32) * keep
    weights = coarse_out.astype(jnp.bfloat16).reshape(count, NEV)

    def solve(index):
        box, row_index, column_index = extended_box(index)
        blocks = factors[row_index, column_index].astype(jnp.float32)
        flat = box.astype(jnp.float32).reshape(NB, BLOCK)
        solved = jnp.einsum("bij,bj->bi", blocks, flat).astype(jnp.bfloat16)
        local_part = jnp.einsum("bij,bi->bj", blocks, solved.astype(jnp.float32)).reshape(ext_rows, ext_columns)
        vectors = basis[row_index, column_index].astype(jnp.float32)
        return local_part + jnp.einsum("k,kxy->xy", weights[index].astype(jnp.float32), vectors)

    totals = lax.map(solve, indices)

    def accumulate(index, accumulated):
        index = jnp.asarray(index).astype(jnp.int32)
        row_index = (index // SUBY).astype(jnp.int32)
        column_index = (index % SUBY).astype(jnp.int32)
        current = lax.dynamic_slice(accumulated, (row_index * CX, column_index * CY), (ext_rows, ext_columns))
        return lax.dynamic_update_slice(accumulated, current + totals[index], (row_index * CX, column_index * CY))

    accumulated = lax.fori_loop(0, count, accumulate, jnp.zeros((NX + 2 * OV, NY + 2 * OV), jnp.float32))
    return accumulated[OV:OV + NX, OV:OV + NY]


def reference(right_side, class_map, class_values, kept_counts, factors, basis, coarse_factor):
    faces = coefficients(class_values[class_map])
    keep = (jnp.arange(NEV, dtype=jnp.int32)[None, None, :] < kept_counts[:, :, None]).astype(jnp.float32).reshape(-1)
    solution_field = jnp.zeros_like(right_side)
    residual = right_side
    preconditioned = precondition(residual, factors, basis, coarse_factor, keep)
    energy = jnp.sum(residual * preconditioned)
    direction = preconditioned
    for step in range(ITERS):
        image = operate(direction, faces)
        step_length = energy / jnp.sum(direction * image)
        solution_field = solution_field + step_length * direction
        residual = residual - step_length * image
        preconditioned = precondition(residual, factors, basis, coarse_factor, keep)
        if step + 1 < ITERS:
            fresh = jnp.sum(residual * preconditioned)
            direction = preconditioned + (fresh / energy) * direction
            energy = fresh
    return solution_field, residual, preconditioned
```

```python
import functools

import jax
import jax.numpy as jnp
from jax import lax
from jax.experimental import pallas as pl
from jax.experimental.pallas import tpu as pltpu
from jax.sharding import PartitionSpec as P

OV = 8
ITERS = 3
LANES = 128
MODES = 32
MESH = pl.DeviceIdType.MESH
SIDES = tuple((a, b) for a in (-1, 0, 1) for b in (-1, 0, 1) if (a, b) != (0, 0))
NT = (((1,), (1,)), ((), ()))
NN = (((1,), (0,)), ((), ()))


def kernel(
    shape,
    right_ref,
    class_ref,
    values_ref,
    kept_ref,
    factors_ref,
    basis_ref,
    coarse_ref,
    field_out,
    residual_out,
    pre_out,
    cond,
    frames,
    fold,
    total,
    natural,
    flat,
    solved,
    message,
    terms,
    gathered,
    scattered,
    halo_send,
    halo_recv,
    fold_send,
    fold_recv,
    gather_send,
    gather_recv,
    scatter_send,
    scatter_recv,
):
    nx, ny = shape
    count = nx * ny
    rows, columns = right_ref.shape
    blocks, block = factors_ref.shape[:2]
    ext_rows, ext_columns = rows + 2 * OV, columns + 2 * OV
    ax, ay = lax.axis_index("gx"), lax.axis_index("gy")
    me = ax * ny + ay
    own = (pl.ds(rows, rows), pl.ds(columns, columns))

    def place(number):
        return (number // ny, number % ny)

    def present(da, db):
        checks = []
        if da:
            checks.append(ax > 0 if da < 0 else ax < nx - 1)
        if db:
            checks.append(ay > 0 if db < 0 else ay < ny - 1)
        return checks[0] if len(checks) == 1 else jnp.logical_and(*checks)

    def patch(ref, da, db):
        return ref.at[pl.ds((1 + da) * rows, rows), pl.ds((1 + db) * columns, columns)]

    def halo_copy(ref, slot, index):
        da, db = SIDES[index]
        return pltpu.make_async_remote_copy(
            src_ref=patch(ref, 0, 0),
            dst_ref=patch(ref, -da, -db),
            send_sem=halo_send.at[slot, index],
            recv_sem=halo_recv.at[slot, index],
            device_id=(ax + da, ay + db),
            device_id_type=MESH,
        )

    def fold_copy(slot, index):
        da, db = SIDES[index]
        return pltpu.make_async_remote_copy(
            src_ref=patch(total, da, db),
            dst_ref=fold.at[slot, index],
            send_sem=fold_send.at[slot, index],
            recv_sem=fold_recv.at[slot, index],
            device_id=(ax + da, ay + db),
            device_id_type=MESH,
        )

    def start_sides(make):
        for index, (da, db) in enumerate(SIDES):

            @pl.when(present(da, db))
            def _(index=index):
                make(index).start()

    def wait_sides(make):
        for index, (da, db) in enumerate(SIDES):

            @pl.when(present(-da, -db))
            def _(index=index):
                make(index).wait_recv()

    def drain_sides(make):
        for index, (da, db) in enumerate(SIDES):

            @pl.when(present(da, db))
            def _(index=index):
                make(index).wait_send()

    def gather_copy(slot, source, target):
        return pltpu.make_async_remote_copy(
            src_ref=message.at[slot],
            dst_ref=gathered.at[slot, source],
            send_sem=gather_send.at[slot],
            recv_sem=gather_recv.at[slot],
            device_id=place(target),
            device_id_type=MESH,
        )

    def scatter_copy(slot, source, target):
        return pltpu.make_async_remote_copy(
            src_ref=terms.at[slot, target],
            dst_ref=scattered.at[slot, source],
            send_sem=scatter_send.at[slot],
            recv_sem=scatter_recv.at[slot],
            device_id=place(target),
            device_id_type=MESH,
        )

    def everything(ref, send, recv, slot):
        span = ref.at[slot, pl.ds(0, count - 1)]
        return pltpu.make_async_remote_copy(
            src_ref=span,
            dst_ref=span,
            send_sem=send.at[slot],
            recv_sem=recv.at[slot],
            device_id=place(lax.rem(me + 1, count)),
            device_id_type=MESH,
        )

    def others(act):
        def one(offset, carry):
            act(lax.rem(me + offset, count))
            return carry

        lax.fori_loop(1, count, one, 0)

    frames[...] = jnp.zeros_like(frames)
    cond[...] = jnp.zeros_like(cond)
    fold[...] = jnp.zeros_like(fold)
    total[...] = jnp.zeros_like(total)
    natural[...] = jnp.zeros_like(natural)
    right = right_ref[...]
    classes = class_ref[...]
    conductivity = jnp.zeros((rows, columns), jnp.float32)
    for level in range(values_ref.shape[0]):
        conductivity = jnp.where(classes == level, values_ref[level], conductivity)
    cond[own] = conductivity
    frames[(0,) + own] = right

    barrier = pltpu.get_barrier_semaphore()
    others(
        lambda target: pl.semaphore_signal(
            barrier, inc=1, device_id=place(target), device_id_type=MESH
        )
    )
    pl.semaphore_wait(barrier, count - 1)

    start_sides(lambda index: halo_copy(frames.at[0], 0, index))
    start_sides(lambda index: halo_copy(cond, ITERS + 1, index))

    frame_shape = cond.shape
    row_at = lax.broadcasted_iota(jnp.int32, frame_shape, 0) + (ax - 1) * rows
    column_at = lax.broadcasted_iota(jnp.int32, frame_shape, 1) + (ay - 1) * columns
    inside = (row_at >= 0) & (row_at < nx * rows) & (column_at >= 0) & (column_at < ny * columns)
    lane = lax.broadcasted_iota(jnp.int32, (1, LANES), 1)
    keep = jnp.where(lane < kept_ref[...], 1.0, 0.0)
    keep_modes = keep[:, :MODES]

    def lane_value(row, index):
        return jnp.sum(jnp.where(lane == index, row, 0.0), axis=1, keepdims=True)

    def whole_sum(values):
        return jnp.sum(jnp.sum(values, axis=0, keepdims=True), axis=1, keepdims=True)

    def precondition(slot, values, scalars):
        wide = frame_shape[1]
        rolled = pltpu.roll(values, wide - (columns - OV), 1)
        natural[...] = rolled[rows - OV : rows - OV + ext_rows]
        for row in range(ext_rows):
            flat[0:1, ext_columns * row : ext_columns * (row + 1)] = natural[
                row : row + 1, 0:ext_columns
            ]
        box = flat[...].astype(jnp.bfloat16)
        coarse_in = lax.dot_general(
            box, basis_ref[...], NT, preferred_element_type=jnp.float32
        )
        row = jnp.zeros((1, LANES), jnp.float32)
        for index, scalar in enumerate(scalars):
            row = jnp.where(lane == MODES + index, scalar, row)
        message[slot] = row
        message[slot, :, 0:MODES] = coarse_in * keep_modes
        others(lambda target: gather_copy(slot, me, target).start())
        gathered[slot, me] = message[slot]
        for index in range(blocks):
            at = slice(index * block, (index + 1) * block)
            half = lax.dot_general(
                box[:, at], factors_ref[index], NT, preferred_element_type=jnp.float32
            ).astype(jnp.bfloat16)
            solved[0:1, at] = lax.dot_general(
                half, factors_ref[index], NN, preferred_element_type=jnp.float32
            )
        everything(gathered, gather_send, gather_recv, slot).wait_recv()
        sums = jnp.sum(gathered[slot], axis=0)
        everyone = jnp.concatenate(
            [gathered[slot, index] for index in range(count)], axis=1
        ).astype(jnp.bfloat16)
        coarse_mid = lax.dot_general(
            everyone, coarse_ref[...], NT, preferred_element_type=jnp.float32
        )
        mid_half = (coarse_mid * keep_modes).astype(jnp.bfloat16)
        spread = lax.dot_general(
            mid_half, coarse_ref[...], NN, preferred_element_type=jnp.float32
        )
        for index in range(count):
            terms[slot, index] = spread[:, index * LANES : (index + 1) * LANES]
        others(lambda target: scatter_copy(slot, me, target).start())
        scattered[slot, me] = terms[slot, me]
        everything(scattered, scatter_send, scatter_recv, slot).wait_recv()
        coarse_out = jnp.sum(scattered[slot], axis=0) * keep
        weights = coarse_out[:, :MODES].astype(jnp.bfloat16)
        solved[...] += lax.dot_general(
            weights, basis_ref[...], NN, preferred_element_type=jnp.float32
        )
        for row in range(ext_rows):
            natural[row : row + 1, 0:ext_columns] = solved[
                0:1, ext_columns * row : ext_columns * (row + 1)
            ]
        lanes = lax.broadcasted_iota(jnp.int32, natural.shape, 1)
        clean = jnp.where(lanes < ext_columns, natural[...], 0.0)
        total[rows - OV : rows - OV + ext_rows, :] = pltpu.roll(clean, columns - OV, 1)
        copies = functools.partial(fold_copy, slot)
        start_sides(copies)
        result = total[own]
        wait_sides(copies)
        for index in range(len(SIDES)):
            result = result + fold[slot, index]
        drain_sides(copies)
        return result, sums

    copies = lambda index: halo_copy(frames.at[0], 0, index)
    wait_sides(copies)
    drain_sides(copies)
    zero = jnp.zeros((1, 1), jnp.float32)
    z, _ = precondition(0, frames[0], (zero,))

    copies = lambda index: halo_copy(cond, ITERS + 1, index)
    wait_sides(copies)
    drain_sides(copies)
    cells = cond[...]
    face_north = 0.5 * (cells + pltpu.roll(cells, 1, 0))
    face_west = 0.5 * (cells + pltpu.roll(cells, 1, 1))

    def operate(field):
        north = face_north * (field - pltpu.roll(field, 1, 0))
        west = face_west * (field - pltpu.roll(field, 1, 1))
        image = north - pltpu.roll(north, frame_shape[0] - 1, 0)
        image = image + (west - pltpu.roll(west, frame_shape[1] - 1, 1))
        return jnp.where(inside, image, 0.0)

    residual = right
    field = jnp.zeros_like(right)
    direction = image = mapped = None
    energy = curvature = None
    for step in range(1, ITERS + 1):
        frames[(step,) + own] = z
        copies = functools.partial(halo_copy, frames.at[step], step)
        start_sides(copies)
        wait_sides(copies)
        drain_sides(copies)
        applied = operate(frames[step])
        applied_own = applied[rows : 2 * rows, columns : 2 * columns]
        scalars = [whole_sum(residual * z), whole_sum(z * applied_own)]
        if step > 1:
            scalars.append(whole_sum(z * image))
        corrected, sums = precondition(step, applied, scalars)
        fresh, plain = lane_value(sums, MODES), lane_value(sums, MODES + 1)
        if step == 1:
            direction, image, mapped, curvature = z, applied_own, corrected, plain
        else:
            ratio = fresh / energy
            cross = lane_value(sums, MODES + 2)
            curvature = plain + 2.0 * ratio * cross + ratio * ratio * curvature
            direction = z + ratio * direction
            image = applied_own + ratio * image
            mapped = corrected + ratio * mapped
        energy = fresh
        length = energy / curvature
        field = field + length * direction
        residual = residual - length * image
        z = z - length * mapped

    field_out[...] = field
    residual_out[...] = residual
    pre_out[...] = z

    for slot in range(ITERS + 1):
        everything(gathered, gather_send, gather_recv, slot).wait_send()
        everything(terms, scatter_send, scatter_recv, slot).wait_send()


def per_device(
    shape, right_side, class_map, class_values, kept_counts, factors, basis, coarse_factor
):
    count = shape[0] * shape[1]
    rows, columns = right_side.shape
    modes = basis.shape[2]
    blocks, block = factors.shape[2:4]
    cells = blocks * block
    flat_basis = jnp.pad(basis.reshape(modes, cells), ((0, MODES - modes), (0, 0)))
    spaced = coarse_factor.reshape(modes, count, modes)
    spaced = jnp.pad(spaced, ((0, MODES - modes), (0, 0), (0, LANES - modes)))
    spaced = spaced.reshape(MODES, count * LANES)
    steps = ITERS + 1
    frame = (3 * rows, 3 * columns)
    vmem = pl.BlockSpec(memory_space=pltpu.VMEM)
    smem = pl.BlockSpec(memory_space=pltpu.SMEM)
    f32 = jnp.float32
    return pl.pallas_call(
        functools.partial(kernel, shape),
        out_shape=(jax.ShapeDtypeStruct((rows, columns), f32),) * 3,
        in_specs=[vmem, vmem, smem, vmem, vmem, vmem, vmem],
        out_specs=(vmem,) * 3,
        scratch_shapes=[
            pltpu.VMEM(frame, f32),
            pltpu.VMEM((steps,) + frame, f32),
            pltpu.VMEM((steps, len(SIDES), rows, columns), f32),
            pltpu.VMEM(frame, f32),
            pltpu.VMEM((rows + 2 * OV, 3 * columns), f32),
            pltpu.VMEM((1, cells), f32),
            pltpu.VMEM((1, cells), f32),
            pltpu.VMEM((steps, 1, LANES), f32),
            pltpu.VMEM((steps, count, 1, LANES), f32),
            pltpu.VMEM((steps, count, 1, LANES), f32),
            pltpu.VMEM((steps, count, 1, LANES), f32),
            pltpu.SemaphoreType.DMA((steps + 1, len(SIDES))),
            pltpu.SemaphoreType.DMA((steps + 1, len(SIDES))),
            pltpu.SemaphoreType.DMA((steps, len(SIDES))),
            pltpu.SemaphoreType.DMA((steps, len(SIDES))),
            pltpu.SemaphoreType.DMA((steps,)),
            pltpu.SemaphoreType.DMA((steps,)),
            pltpu.SemaphoreType.DMA((steps,)),
            pltpu.SemaphoreType.DMA((steps,)),
        ],
        compiler_params=pltpu.CompilerParams(
            collective_id=0, has_side_effects=True, vmem_limit_bytes=40 * 2**20
        ),
    )(
        right_side,
        class_map,
        class_values,
        kept_counts,
        factors.reshape(blocks, block, block),
        flat_basis,
        spaced,
    )


def solution(mesh):
    shape = (mesh.shape["gx"], mesh.shape["gy"])
    in_specs = (
        P("gx", "gy"),
        P("gx", "gy"),
        P(),
        P("gx", "gy"),
        P("gx", "gy", None, None, None),
        P("gx", "gy", None, None, None),
        P(("gx", "gy"), None),
    )
    out_specs = (P("gx", "gy"), P("gx", "gy"), P("gx", "gy"))

    return jax.shard_map(
        functools.partial(per_device, shape),
        mesh=mesh,
        in_specs=in_specs,
        out_specs=out_specs,
        check_vma=False,
    )
```

```python
import functools

import jax
import jax.numpy as jnp
from jax import lax
from jax.experimental import pallas as pl
from jax.experimental.pallas import tpu as pltpu
from jax.sharding import PartitionSpec as P

OV = 8
ITERS = 3
LANES = 128
MODES = 32
MESH = pl.DeviceIdType.MESH
SIDES = tuple((a, b) for a in (-1, 0, 1) for b in (-1, 0, 1) if (a, b) != (0, 0))
TN = (((0,), (0,)), ((), ()))
NT = (((1,), (1,)), ((), ()))
NN = (((1,), (0,)), ((), ()))


def kernel(
    shape,
    right_in,
    class_in,
    values_ref,
    kept_in,
    factors_in,
    basis_in,
    coarse_in_ref,
    out,
    right_ref,
    class_ref,
    kept_ref,
    factors_ref,
    basis_ref,
    coarse_rows,
    load_sems,
    gram,
    coarse_wide,
    coarse_ref,
    cond,
    frames,
    fold,
    total,
    natural,
    flat,
    solved,
    message,
    terms,
    gathered,
    scattered,
    halo_send,
    halo_recv,
    fold_send,
    fold_recv,
    gather_send,
    gather_recv,
    scatter_send,
    scatter_recv,
):
    nx, ny = shape
    count = nx * ny
    rows, columns = right_ref.shape
    modes = coarse_rows.shape[0]
    blocks, block = factors_ref.shape[:2]
    ext_rows, ext_columns = rows + 2 * OV, columns + 2 * OV
    ax, ay = lax.axis_index("gx"), lax.axis_index("gy")
    me = ax * ny + ay
    own = (pl.ds(rows, rows), pl.ds(columns, columns))

    loads = [
        pltpu.make_async_copy(source, target, load_sems.at[index])
        for index, (source, target) in enumerate(
            (
                (right_in, right_ref),
                (class_in, class_ref),
                (kept_in, kept_ref),
                (coarse_in_ref, coarse_rows),
                (factors_in, factors_ref),
                (basis_in, basis_ref),
            )
        )
    ]
    for load in loads:
        load.start()

    def wrap(value, size):
        return jnp.where(value >= size, value - size, value)

    def present(da, db):
        checks = []
        if da:
            checks.append(ax > 0 if da < 0 else ax < nx - 1)
        if db:
            checks.append(ay > 0 if db < 0 else ay < ny - 1)
        return checks[0] if len(checks) == 1 else jnp.logical_and(*checks)

    def patch(ref, da, db):
        return ref.at[pl.ds((1 + da) * rows, rows), pl.ds((1 + db) * columns, columns)]

    def halo_copy(ref, slot, index):
        da, db = SIDES[index]
        return pltpu.make_async_remote_copy(
            src_ref=patch(ref, 0, 0),
            dst_ref=patch(ref, -da, -db),
            send_sem=halo_send.at[slot, index],
            recv_sem=halo_recv.at[slot, index],
            device_id=(ax + da, ay + db),
            device_id_type=MESH,
        )

    def fold_copy(slot, index):
        da, db = SIDES[index]
        first, extent = (rows - OV if da < 0 else 0), (OV if da else rows)
        lanes = pl.ds((1 + db) * columns, columns)
        return pltpu.make_async_remote_copy(
            src_ref=total.at[slot, pl.ds((1 + da) * rows + first, extent), lanes],
            dst_ref=fold.at[slot, index, pl.ds(first, extent)],
            send_sem=fold_send.at[slot, index],
            recv_sem=fold_recv.at[slot, index],
            device_id=(ax + da, ay + db),
            device_id_type=MESH,
        )

    def start_sides(make):
        for index, (da, db) in enumerate(SIDES):

            @pl.when(present(da, db))
            def _(index=index):
                make(index).start()

    def wait_sides(make):
        for index, (da, db) in enumerate(SIDES):

            @pl.when(present(-da, -db))
            def _(index=index):
                make(index).wait_recv()

    def drain_sides(make):
        for index, (da, db) in enumerate(SIDES):

            @pl.when(present(da, db))
            def _(index=index):
                make(index).wait_send()

    def gather_copy(slot, tx, ty):
        return pltpu.make_async_remote_copy(
            src_ref=message.at[slot],
            dst_ref=gathered.at[slot, me],
            send_sem=gather_send.at[slot],
            recv_sem=gather_recv.at[slot],
            device_id=(tx, ty),
            device_id_type=MESH,
        )

    def scatter_copy(slot, tx, ty):
        return pltpu.make_async_remote_copy(
            src_ref=terms.at[slot, tx * ny + ty],
            dst_ref=scattered.at[slot, me],
            send_sem=scatter_send.at[slot],
            recv_sem=scatter_recv.at[slot],
            device_id=(tx, ty),
            device_id_type=MESH,
        )

    def everything(ref, send, recv, slot):
        span = ref.at[slot, pl.ds(0, count - 1)]
        return pltpu.make_async_remote_copy(
            src_ref=span,
            dst_ref=span,
            send_sem=send.at[slot],
            recv_sem=recv.at[slot],
            device_id=(wrap(ax + 1, nx), ay),
            device_id_type=MESH,
        )

    def others(act):
        columns_of = [ay] + [wrap(ay + step, ny) for step in range(1, ny)]
        for ty in columns_of[1:]:
            act(ax, ty)

        def one(offset, carry):
            tx = wrap(ax + offset, nx)
            for ty in columns_of:
                act(tx, ty)
            return carry

        lax.fori_loop(1, nx, one, 0)

    frames[...] = jnp.zeros_like(frames)
    cond[...] = jnp.zeros_like(cond)
    fold[...] = jnp.zeros_like(fold)
    total[...] = jnp.zeros_like(total)
    barrier = pltpu.get_barrier_semaphore()
    others(
        lambda tx, ty: pl.semaphore_signal(
            barrier, inc=1, device_id=(tx, ty), device_id_type=MESH
        )
    )
    natural[...] = jnp.zeros_like(natural)
    for load in loads[:4]:
        load.wait()
    right = right_ref[...]
    classes = class_ref[...]
    conductivity = jnp.zeros((rows, columns), jnp.float32)
    for level in range(values_ref.shape[0]):
        conductivity = jnp.where(classes == level, values_ref[level], conductivity)
    cond[own] = conductivity
    frames[(0,) + own] = right
    coarse_wide[...] = jnp.zeros_like(coarse_wide)
    narrow = coarse_rows[...].astype(jnp.float32)
    for index in range(count):
        coarse_wide[0:modes, index * LANES : index * LANES + modes] = narrow[
            :, index * modes : (index + 1) * modes
        ]
    coarse_ref[...] = coarse_wide[...].astype(jnp.bfloat16)
    pl.semaphore_wait(barrier, count - 1)

    start_sides(lambda index: halo_copy(frames.at[0], 0, index))
    start_sides(lambda index: halo_copy(cond, ITERS + 1, index))
    for load in loads[4:]:
        load.wait()
    for index in range(blocks):
        factor = factors_ref[index]
        gram[index] = lax.dot_general(
            factor, factor, TN, preferred_element_type=jnp.float32
        ).astype(jnp.bfloat16)

    frame_shape = cond.shape
    row_at = lax.broadcasted_iota(jnp.int32, frame_shape, 0) + (ax - 1) * rows
    column_at = lax.broadcasted_iota(jnp.int32, frame_shape, 1) + (ay - 1) * columns
    inside = (row_at >= 0) & (row_at < nx * rows) & (column_at >= 0) & (column_at < ny * columns)
    lane = lax.broadcasted_iota(jnp.int32, (1, LANES), 1)
    keep = jnp.where(lane < kept_ref[...], 1.0, 0.0)
    keep_modes = keep[:, :MODES]

    def lane_value(row, index):
        return jnp.sum(jnp.where(lane == index, row, 0.0), axis=1, keepdims=True)

    def whole_sum(values):
        return jnp.sum(jnp.sum(values, axis=0, keepdims=True), axis=1, keepdims=True)

    def precondition(slot, values, scalars):
        wide = frame_shape[1]
        rolled = pltpu.roll(values, wide - (columns - OV), 1)
        natural[...] = rolled[rows - OV : rows - OV + ext_rows]
        for row in range(ext_rows):
            flat[0:1, ext_columns * row : ext_columns * (row + 1)] = natural[
                row : row + 1, 0:ext_columns
            ]
        box = flat[...].astype(jnp.bfloat16)
        coarse_in = lax.dot_general(
            box, basis_ref[...], NT, preferred_element_type=jnp.float32
        )
        row = jnp.zeros((1, LANES), jnp.float32)
        for index, scalar in enumerate(scalars):
            row = jnp.where(lane == MODES + index, scalar, row)
        message[slot] = row
        message[slot, :, 0:MODES] = coarse_in * keep_modes
        others(lambda tx, ty: gather_copy(slot, tx, ty).start())
        gathered[slot, me] = message[slot]
        for index in range(blocks):
            at = slice(index * block, (index + 1) * block)
            solved[0:1, at] = lax.dot_general(
                box[:, at], gram[index], NN, preferred_element_type=jnp.float32
            )
        everything(gathered, gather_send, gather_recv, slot).wait_recv()
        sums = jnp.sum(gathered[slot], axis=0)
        everyone = jnp.concatenate(
            [gathered[slot, index] for index in range(count)], axis=1
        ).astype(jnp.bfloat16)
        coarse_mid = lax.dot_general(
            everyone, coarse_ref[...], NT, preferred_element_type=jnp.float32
        )
        mid_half = (coarse_mid * keep_modes).astype(jnp.bfloat16)
        spread = lax.dot_general(
            mid_half, coarse_ref[...], NN, preferred_element_type=jnp.float32
        )
        for index in range(count):
            terms[slot, index] = spread[:, index * LANES : (index + 1) * LANES]
        others(lambda tx, ty: scatter_copy(slot, tx, ty).start())
        scattered[slot, me] = terms[slot, me]
        everything(scattered, scatter_send, scatter_recv, slot).wait_recv()
        coarse_out = jnp.sum(scattered[slot], axis=0) * keep
        weights = coarse_out[:, :MODES].astype(jnp.bfloat16)
        solved[...] += lax.dot_general(
            weights, basis_ref[...], NN, preferred_element_type=jnp.float32
        )
        for row in range(ext_rows):
            natural[row : row + 1, 0:ext_columns] = solved[
                0:1, ext_columns * row : ext_columns * (row + 1)
            ]
        lanes = lax.broadcasted_iota(jnp.int32, natural.shape, 1)
        clean = jnp.where(lanes < ext_columns, natural[...], 0.0)
        total[slot, rows - OV : rows - OV + ext_rows, :] = pltpu.roll(clean, columns - OV, 1)
        copies = functools.partial(fold_copy, slot)
        start_sides(copies)
        result = total[(slot,) + own]
        wait_sides(copies)
        for index in range(len(SIDES)):
            result = result + fold[slot, index]
        return result, sums

    copies = lambda index: halo_copy(frames.at[0], 0, index)
    wait_sides(copies)
    zero = jnp.zeros((1, 1), jnp.float32)
    z, _ = precondition(0, frames[0], (zero,))

    copies = lambda index: halo_copy(cond, ITERS + 1, index)
    wait_sides(copies)
    cells = cond[...]
    face_north = 0.5 * (cells + pltpu.roll(cells, 1, 0))
    face_west = 0.5 * (cells + pltpu.roll(cells, 1, 1))

    def operate(field):
        north = face_north * (field - pltpu.roll(field, 1, 0))
        west = face_west * (field - pltpu.roll(field, 1, 1))
        image = north - pltpu.roll(north, frame_shape[0] - 1, 0)
        image = image + (west - pltpu.roll(west, frame_shape[1] - 1, 1))
        return jnp.where(inside, image, 0.0)

    residual = right
    field = jnp.zeros_like(right)
    direction = image = mapped = None
    energy = curvature = None
    for step in range(1, ITERS + 1):
        frames[(step,) + own] = z
        copies = functools.partial(halo_copy, frames.at[step], step)
        start_sides(copies)
        wait_sides(copies)
        applied = operate(frames[step])
        applied_own = applied[rows : 2 * rows, columns : 2 * columns]
        scalars = [whole_sum(residual * z), whole_sum(z * applied_own)]
        if step > 1:
            scalars.append(whole_sum(z * image))
        corrected, sums = precondition(step, applied, scalars)
        fresh, plain = lane_value(sums, MODES), lane_value(sums, MODES + 1)
        if step == 1:
            direction, image, mapped, curvature = z, applied_own, corrected, plain
        else:
            ratio = fresh / energy
            cross = lane_value(sums, MODES + 2)
            curvature = plain + 2.0 * ratio * cross + ratio * ratio * curvature
            direction = z + ratio * direction
            image = applied_own + ratio * image
            mapped = corrected + ratio * mapped
        energy = fresh
        length = energy / curvature
        field = field + length * direction
        residual = residual - length * image
        z = z - length * mapped

    out[0] = field
    out[1] = residual
    out[2] = z
    drain_sides(lambda index: halo_copy(cond, ITERS + 1, index))

    for slot in range(ITERS + 1):
        everything(gathered, gather_send, gather_recv, slot).wait_send()
        everything(terms, scatter_send, scatter_recv, slot).wait_send()
        drain_sides(functools.partial(halo_copy, frames.at[slot], slot))
        drain_sides(functools.partial(fold_copy, slot))


def per_device(
    shape, right_side, class_map, class_values, kept_counts, factors, basis, coarse_factor
):
    count = shape[0] * shape[1]
    rows, columns = right_side.shape
    modes = basis.shape[2]
    blocks, block = factors.shape[2:4]
    cells = blocks * block
    flat_basis = jnp.pad(basis.reshape(modes, cells), ((0, MODES - modes), (0, 0)))
    steps = ITERS + 1
    frame = (3 * rows, 3 * columns)
    vmem = pl.BlockSpec(memory_space=pltpu.VMEM)
    hbm = pl.BlockSpec(memory_space=pltpu.HBM)
    smem = pl.BlockSpec(memory_space=pltpu.SMEM)
    f32, half = jnp.float32, jnp.bfloat16
    stacked = pl.pallas_call(
        functools.partial(kernel, shape),
        out_shape=jax.ShapeDtypeStruct((3, rows, columns), f32),
        in_specs=[hbm, hbm, smem, hbm, hbm, hbm, hbm],
        out_specs=vmem,
        scratch_shapes=[
            pltpu.VMEM((rows, columns), f32),
            pltpu.VMEM((rows, columns), jnp.int32),
            pltpu.VMEM((1, 1), jnp.int32),
            pltpu.VMEM((blocks, block, block), half),
            pltpu.VMEM((MODES, cells), half),
            pltpu.VMEM(coarse_factor.shape, half),
            pltpu.SemaphoreType.DMA((6,)),
            pltpu.VMEM((blocks, block, block), half),
            pltpu.VMEM((MODES, count * LANES), f32),
            pltpu.VMEM((MODES, count * LANES), half),
            pltpu.VMEM(frame, f32),
            pltpu.VMEM((steps,) + frame, f32),
            pltpu.VMEM((steps, len(SIDES), rows, columns), f32),
            pltpu.VMEM((steps,) + frame, f32),
            pltpu.VMEM((rows + 2 * OV, 3 * columns), f32),
            pltpu.VMEM((1, cells), f32),
            pltpu.VMEM((1, cells), f32),
            pltpu.VMEM((steps, 1, LANES), f32),
            pltpu.VMEM((steps, count, 1, LANES), f32),
            pltpu.VMEM((steps, count, 1, LANES), f32),
            pltpu.VMEM((steps, count, 1, LANES), f32),
            pltpu.SemaphoreType.DMA((steps + 1, len(SIDES))),
            pltpu.SemaphoreType.DMA((steps + 1, len(SIDES))),
            pltpu.SemaphoreType.DMA((steps, len(SIDES))),
            pltpu.SemaphoreType.DMA((steps, len(SIDES))),
            pltpu.SemaphoreType.DMA((steps,)),
            pltpu.SemaphoreType.DMA((steps,)),
            pltpu.SemaphoreType.DMA((steps,)),
            pltpu.SemaphoreType.DMA((steps,)),
        ],
        compiler_params=pltpu.CompilerParams(
            collective_id=0, has_side_effects=True, vmem_limit_bytes=40 * 2**20
        ),
    )(
        right_side,
        class_map,
        class_values,
        kept_counts,
        factors.reshape(blocks, block, block),
        flat_basis,
        coarse_factor,
    )
    return (stacked[0], stacked[1], stacked[2])


def solution(mesh):
    shape = (mesh.shape["gx"], mesh.shape["gy"])
    in_specs = (
        P("gx", "gy"),
        P("gx", "gy"),
        P(),
        P("gx", "gy"),
        P("gx", "gy", None, None, None),
        P("gx", "gy", None, None, None),
        P(("gx", "gy"), None),
    )
    out_specs = (P("gx", "gy"), P("gx", "gy"), P("gx", "gy"))

    return jax.shard_map(
        functools.partial(per_device, shape),
        mesh=mesh,
        in_specs=in_specs,
        out_specs=out_specs,
        check_vma=False,
    )
```

```python
import functools

import jax
import jax.numpy as jnp
from jax import lax
from jax.experimental import pallas as pl
from jax.experimental.pallas import tpu as pltpu
from jax.sharding import PartitionSpec as P

OV = 8
ITERS = 3
LANES = 128
MODES = 32
MESH = pl.DeviceIdType.MESH
SIDES = tuple((a, b) for a in (-1, 0, 1) for b in (-1, 0, 1) if (a, b) != (0, 0))
TN = (((0,), (0,)), ((), ()))
NT = (((1,), (1,)), ((), ()))
NN = (((1,), (0,)), ((), ()))


def kernel(
    shape,
    right_in,
    class_in,
    values_ref,
    kept_in,
    factors_in,
    basis_in,
    coarse_in_ref,
    out,
    right_ref,
    class_ref,
    kept_ref,
    factors_ref,
    basis_ref,
    coarse_rows,
    load_sems,
    gram,
    coarse_wide,
    coarse_ref,
    cond,
    frames,
    fold,
    total,
    natural,
    flat,
    solved,
    message,
    terms,
    gathered,
    scattered,
    halo_send,
    halo_recv,
    fold_send,
    fold_recv,
    gather_send,
    gather_recv,
    scatter_send,
    scatter_recv,
):
    nx, ny = shape
    count = nx * ny
    rows, columns = right_ref.shape
    modes = coarse_rows.shape[0]
    blocks, block = factors_ref.shape[:2]
    ext_rows, ext_columns = rows + 2 * OV, columns + 2 * OV
    ax, ay = lax.axis_index("gx"), lax.axis_index("gy")
    me = ax * ny + ay
    own = (pl.ds(rows, rows), pl.ds(columns, columns))

    loads = [
        pltpu.make_async_copy(source, target, load_sems.at[index])
        for index, (source, target) in enumerate(
            (
                (right_in, right_ref),
                (class_in, class_ref),
                (kept_in, kept_ref),
                (coarse_in_ref, coarse_rows),
                (factors_in, factors_ref),
                (basis_in, basis_ref),
            )
        )
    ]
    for load in loads:
        load.start()

    def wrap(value, size):
        return jnp.where(value >= size, value - size, value)

    def present(da, db):
        checks = []
        if da:
            checks.append(ax > 0 if da < 0 else ax < nx - 1)
        if db:
            checks.append(ay > 0 if db < 0 else ay < ny - 1)
        return checks[0] if len(checks) == 1 else jnp.logical_and(*checks)

    def patch(ref, da, db):
        return ref.at[pl.ds((1 + da) * rows, rows), pl.ds((1 + db) * columns, columns)]

    def halo_copy(ref, slot, index):
        da, db = SIDES[index]
        return pltpu.make_async_remote_copy(
            src_ref=patch(ref, 0, 0),
            dst_ref=patch(ref, -da, -db),
            send_sem=halo_send.at[slot, index],
            recv_sem=halo_recv.at[slot, index],
            device_id=(ax + da, ay + db),
            device_id_type=MESH,
        )

    def fold_copy(slot, index):
        da, db = SIDES[index]
        first, extent = (rows - OV if da < 0 else 0), (OV if da else rows)
        lanes = pl.ds((1 + db) * columns, columns)
        return pltpu.make_async_remote_copy(
            src_ref=total.at[slot, pl.ds((1 + da) * rows + first, extent), lanes],
            dst_ref=fold.at[slot, index, pl.ds(first, extent)],
            send_sem=fold_send.at[slot, index],
            recv_sem=fold_recv.at[slot, index],
            device_id=(ax + da, ay + db),
            device_id_type=MESH,
        )

    def start_sides(make):
        for index, (da, db) in enumerate(SIDES):

            @pl.when(present(da, db))
            def _(index=index):
                make(index).start()

    def wait_sides(make):
        for index, (da, db) in enumerate(SIDES):

            @pl.when(present(-da, -db))
            def _(index=index):
                make(index).wait_recv()

    def drain_sides(make):
        for index, (da, db) in enumerate(SIDES):

            @pl.when(present(da, db))
            def _(index=index):
                make(index).wait_send()

    def gather_copy(slot, tx, ty):
        return pltpu.make_async_remote_copy(
            src_ref=message.at[slot],
            dst_ref=gathered.at[slot, me],
            send_sem=gather_send.at[slot],
            recv_sem=gather_recv.at[slot],
            device_id=(tx, ty),
            device_id_type=MESH,
        )

    def scatter_copy(slot, tx, ty):
        return pltpu.make_async_remote_copy(
            src_ref=terms.at[slot, tx * ny + ty],
            dst_ref=scattered.at[slot, me],
            send_sem=scatter_send.at[slot],
            recv_sem=scatter_recv.at[slot],
            device_id=(tx, ty),
            device_id_type=MESH,
        )

    def everything(ref, send, recv, slot):
        span = ref.at[slot, pl.ds(0, count - 1)]
        return pltpu.make_async_remote_copy(
            src_ref=span,
            dst_ref=span,
            send_sem=send.at[slot],
            recv_sem=recv.at[slot],
            device_id=(wrap(ax + 1, nx), ay),
            device_id_type=MESH,
        )

    def others(act):
        columns_of = [ay] + [wrap(ay + step, ny) for step in range(1, ny)]
        def one(offset, carry):
            tx = wrap(ax + offset, nx)
            for ty in columns_of:
                act(tx, ty)
            return carry

        lax.fori_loop(1, nx, one, 0, unroll=nx - 1 if nx <= 8 else 1)
        for ty in columns_of[1:]:
            act(ax, ty)

    frames[...] = jnp.zeros_like(frames)
    cond[...] = jnp.zeros_like(cond)
    fold[...] = jnp.zeros_like(fold)
    total[...] = jnp.zeros_like(total)
    barrier = pltpu.get_barrier_semaphore()
    others(
        lambda tx, ty: pl.semaphore_signal(
            barrier, inc=1, device_id=(tx, ty), device_id_type=MESH
        )
    )
    natural[...] = jnp.zeros_like(natural)
    for load in loads[:4]:
        load.wait()
    right = right_ref[...]
    classes = class_ref[...]
    conductivity = jnp.zeros((rows, columns), jnp.float32)
    for level in range(values_ref.shape[0]):
        conductivity = jnp.where(classes == level, values_ref[level], conductivity)
    cond[own] = conductivity
    frames[(0,) + own] = right
    coarse_wide[...] = jnp.zeros_like(coarse_wide)
    narrow = coarse_rows[...].astype(jnp.float32)
    for index in range(count):
        coarse_wide[0:modes, index * LANES : index * LANES + modes] = narrow[
            :, index * modes : (index + 1) * modes
        ]
    coarse_ref[...] = coarse_wide[...].astype(jnp.bfloat16)
    pl.semaphore_wait(barrier, count - 1)

    start_sides(lambda index: halo_copy(frames.at[0], 0, index))
    start_sides(lambda index: halo_copy(cond, ITERS + 1, index))
    for load in loads[4:]:
        load.wait()
    for index in range(blocks):
        factor = factors_ref[index]
        gram[index] = lax.dot_general(
            factor, factor, TN, preferred_element_type=jnp.float32
        ).astype(jnp.bfloat16)

    frame_shape = cond.shape
    row_at = lax.broadcasted_iota(jnp.int32, frame_shape, 0) + (ax - 1) * rows
    column_at = lax.broadcasted_iota(jnp.int32, frame_shape, 1) + (ay - 1) * columns
    inside = (row_at >= 0) & (row_at < nx * rows) & (column_at >= 0) & (column_at < ny * columns)
    lane = lax.broadcasted_iota(jnp.int32, (1, LANES), 1)
    keep = jnp.where(lane < kept_ref[...], 1.0, 0.0)
    keep_modes = keep[:, :MODES]

    def lane_value(row, index):
        return jnp.sum(jnp.where(lane == index, row, 0.0), axis=1, keepdims=True)

    def whole_sum(values):
        return jnp.sum(jnp.sum(values, axis=0, keepdims=True), axis=1, keepdims=True)

    def precondition(slot, values, pairs):
        wide = frame_shape[1]
        rolled = pltpu.roll(values, wide - (columns - OV), 1)
        natural[...] = rolled[rows - OV : rows - OV + ext_rows]
        for row in range(ext_rows):
            flat[0:1, ext_columns * row : ext_columns * (row + 1)] = natural[
                row : row + 1, 0:ext_columns
            ]
        box = flat[...].astype(jnp.bfloat16)
        coarse_in = lax.dot_general(
            box, basis_ref[...], NT, preferred_element_type=jnp.float32
        )
        message[slot] = jnp.zeros((1, LANES), jnp.float32)
        message[slot, :, 0:MODES] = coarse_in * keep_modes
        others(lambda tx, ty: gather_copy(slot, tx, ty).start())
        gathered[slot, me] = message[slot]
        shares = jnp.zeros((1, LANES), jnp.float32)
        for index, (first, second) in enumerate(pairs):
            shares = jnp.where(lane == MODES + index, whole_sum(first * second), shares)
        for index in range(blocks):
            at = slice(index * block, (index + 1) * block)
            solved[0:1, at] = lax.dot_general(
                box[:, at], gram[index], NN, preferred_element_type=jnp.float32
            )
        everything(gathered, gather_send, gather_recv, slot).wait_recv()
        everyone = jnp.concatenate(
            [gathered[slot, index] for index in range(count)], axis=1
        ).astype(jnp.bfloat16)
        coarse_mid = lax.dot_general(
            everyone, coarse_ref[...], NT, preferred_element_type=jnp.float32
        )
        mid_half = (coarse_mid * keep_modes).astype(jnp.bfloat16)
        spread = lax.dot_general(
            mid_half, coarse_ref[...], NN, preferred_element_type=jnp.float32
        )
        for index in range(count):
            terms[slot, index] = spread[:, index * LANES : (index + 1) * LANES] + shares
        others(lambda tx, ty: scatter_copy(slot, tx, ty).start())
        scattered[slot, me] = terms[slot, me]
        everything(scattered, scatter_send, scatter_recv, slot).wait_recv()
        sums = jnp.sum(scattered[slot], axis=0)
        coarse_out = sums * keep
        weights = coarse_out[:, :MODES].astype(jnp.bfloat16)
        solved[...] += lax.dot_general(
            weights, basis_ref[...], NN, preferred_element_type=jnp.float32
        )
        for row in range(ext_rows):
            natural[row : row + 1, 0:ext_columns] = solved[
                0:1, ext_columns * row : ext_columns * (row + 1)
            ]
        lanes = lax.broadcasted_iota(jnp.int32, natural.shape, 1)
        clean = jnp.where(lanes < ext_columns, natural[...], 0.0)
        total[slot, rows - OV : rows - OV + ext_rows, :] = pltpu.roll(clean, columns - OV, 1)
        copies = functools.partial(fold_copy, slot)
        start_sides(copies)
        result = total[(slot,) + own]
        wait_sides(copies)
        for index in range(len(SIDES)):
            result = result + fold[slot, index]
        return result, sums

    copies = lambda index: halo_copy(frames.at[0], 0, index)
    wait_sides(copies)
    z, _ = precondition(0, frames[0], ())

    copies = lambda index: halo_copy(cond, ITERS + 1, index)
    wait_sides(copies)
    cells = cond[...]
    face_north = 0.5 * (cells + pltpu.roll(cells, 1, 0))
    face_west = 0.5 * (cells + pltpu.roll(cells, 1, 1))

    def operate(field):
        north = face_north * (field - pltpu.roll(field, 1, 0))
        west = face_west * (field - pltpu.roll(field, 1, 1))
        image = north - pltpu.roll(north, frame_shape[0] - 1, 0)
        image = image + (west - pltpu.roll(west, frame_shape[1] - 1, 1))
        return jnp.where(inside, image, 0.0)

    residual = right
    field = jnp.zeros_like(right)
    direction = image = mapped = None
    energy = curvature = None
    for step in range(1, ITERS + 1):
        frames[(step,) + own] = z
        copies = functools.partial(halo_copy, frames.at[step], step)
        start_sides(copies)
        wait_sides(copies)
        applied = operate(frames[step])
        applied_own = applied[rows : 2 * rows, columns : 2 * columns]
        pairs = [(residual, z), (z, applied_own)]
        if step > 1:
            pairs.append((z, image))
        corrected, sums = precondition(step, applied, pairs)
        fresh, plain = lane_value(sums, MODES), lane_value(sums, MODES + 1)
        if step == 1:
            direction, image, mapped, curvature = z, applied_own, corrected, plain
        else:
            ratio = fresh / energy
            cross = lane_value(sums, MODES + 2)
            curvature = plain + 2.0 * ratio * cross + ratio * ratio * curvature
            direction = z + ratio * direction
            image = applied_own + ratio * image
            mapped = corrected + ratio * mapped
        energy = fresh
        length = energy / curvature
        field = field + length * direction
        residual = residual - length * image
        z = z - length * mapped

    out[0] = field
    out[1] = residual
    out[2] = z
    drain_sides(lambda index: halo_copy(cond, ITERS + 1, index))

    for slot in range(ITERS + 1):
        everything(gathered, gather_send, gather_recv, slot).wait_send()
        everything(terms, scatter_send, scatter_recv, slot).wait_send()
        drain_sides(functools.partial(halo_copy, frames.at[slot], slot))
        drain_sides(functools.partial(fold_copy, slot))


def per_device(
    shape, right_side, class_map, class_values, kept_counts, factors, basis, coarse_factor
):
    count = shape[0] * shape[1]
    rows, columns = right_side.shape
    modes = basis.shape[2]
    blocks, block = factors.shape[2:4]
    cells = blocks * block
    flat_basis = jnp.pad(basis.reshape(modes, cells), ((0, MODES - modes), (0, 0)))
    steps = ITERS + 1
    frame = (3 * rows, 3 * columns)
    vmem = pl.BlockSpec(memory_space=pltpu.VMEM)
    hbm = pl.BlockSpec(memory_space=pltpu.HBM)
    smem = pl.BlockSpec(memory_space=pltpu.SMEM)
    f32, half = jnp.float32, jnp.bfloat16
    stacked = pl.pallas_call(
        functools.partial(kernel, shape),
        out_shape=jax.ShapeDtypeStruct((3, rows, columns), f32),
        in_specs=[hbm, hbm, smem, hbm, hbm, hbm, hbm],
        out_specs=vmem,
        scratch_shapes=[
            pltpu.VMEM((rows, columns), f32),
            pltpu.VMEM((rows, columns), jnp.int32),
            pltpu.VMEM((1, 1), jnp.int32),
            pltpu.VMEM((blocks, block, block), half),
            pltpu.VMEM((MODES, cells), half),
            pltpu.VMEM(coarse_factor.shape, half),
            pltpu.SemaphoreType.DMA((6,)),
            pltpu.VMEM((blocks, block, block), half),
            pltpu.VMEM((MODES, count * LANES), f32),
            pltpu.VMEM((MODES, count * LANES), half),
            pltpu.VMEM(frame, f32),
            pltpu.VMEM((steps,) + frame, f32),
            pltpu.VMEM((steps, len(SIDES), rows, columns), f32),
            pltpu.VMEM((steps,) + frame, f32),
            pltpu.VMEM((rows + 2 * OV, 3 * columns), f32),
            pltpu.VMEM((1, cells), f32),
            pltpu.VMEM((1, cells), f32),
            pltpu.VMEM((steps, 1, LANES), f32),
            pltpu.VMEM((steps, count, 1, LANES), f32),
            pltpu.VMEM((steps, count, 1, LANES), f32),
            pltpu.VMEM((steps, count, 1, LANES), f32),
            pltpu.SemaphoreType.DMA((steps + 1, len(SIDES))),
            pltpu.SemaphoreType.DMA((steps + 1, len(SIDES))),
            pltpu.SemaphoreType.DMA((steps, len(SIDES))),
            pltpu.SemaphoreType.DMA((steps, len(SIDES))),
            pltpu.SemaphoreType.DMA((steps,)),
            pltpu.SemaphoreType.DMA((steps,)),
            pltpu.SemaphoreType.DMA((steps,)),
            pltpu.SemaphoreType.DMA((steps,)),
        ],
        compiler_params=pltpu.CompilerParams(
            collective_id=0, has_side_effects=True, vmem_limit_bytes=60 * 2**20
        ),
    )(
        right_side,
        class_map,
        class_values,
        kept_counts,
        factors.reshape(blocks, block, block),
        flat_basis,
        coarse_factor,
    )
    return (stacked[0], stacked[1], stacked[2])


def solution(mesh):
    shape = (mesh.shape["gx"], mesh.shape["gy"])
    in_specs = (
        P("gx", "gy"),
        P("gx", "gy"),
        P(),
        P("gx", "gy"),
        P("gx", "gy", None, None, None),
        P("gx", "gy", None, None, None),
        P(("gx", "gy"), None),
    )
    out_specs = (P("gx", "gy"), P("gx", "gy"), P("gx", "gy"))

    return jax.shard_map(
        functools.partial(per_device, shape),
        mesh=mesh,
        in_specs=in_specs,
        out_specs=out_specs,
        check_vma=False,
    )
```

```python
import functools

import jax
import jax.numpy as jnp
from jax import lax
from jax.experimental import pallas as pl
from jax.experimental.pallas import tpu as pltpu
from jax.sharding import PartitionSpec as P

OV = 8
ITERS = 3
LANES = 128
MODES = 32
MESH = pl.DeviceIdType.MESH
SIDES = tuple((a, b) for a in (-1, 0, 1) for b in (-1, 0, 1) if (a, b) != (0, 0))
TN = (((0,), (0,)), ((), ()))
NT = (((1,), (1,)), ((), ()))
NN = (((1,), (0,)), ((), ()))


def kernel(
    shape,
    right_in,
    class_in,
    values_ref,
    kept_in,
    factors_in,
    basis_in,
    coarse_in_ref,
    out,
    right_ref,
    class_ref,
    kept_ref,
    factors_ref,
    basis_ref,
    coarse_rows,
    load_sems,
    gram,
    coarse_wide,
    coarse_ref,
    cond,
    frames,
    fold,
    total,
    natural,
    flat,
    solved,
    message,
    terms,
    gathered,
    scattered,
    halo_send,
    halo_recv,
    fold_send,
    fold_recv,
    gather_send,
    gather_recv,
    scatter_send,
    scatter_recv,
):
    nx, ny = shape
    count = nx * ny
    rows, columns = right_ref.shape
    modes = coarse_rows.shape[0]
    blocks, block = factors_ref.shape[:2]
    ext_rows, ext_columns = rows + 2 * OV, columns + 2 * OV
    ax, ay = lax.axis_index("gx"), lax.axis_index("gy")
    me = ax * ny + ay
    own = (pl.ds(rows, rows), pl.ds(columns, columns))

    loads = [
        pltpu.make_async_copy(source, target, load_sems.at[index])
        for index, (source, target) in enumerate(
            (
                (right_in, right_ref),
                (class_in, class_ref),
                (kept_in, kept_ref),
                (coarse_in_ref, coarse_rows),
                (factors_in, factors_ref),
                (basis_in, basis_ref),
            )
        )
    ]
    for load in loads:
        load.start()

    def wrap(value, size):
        return jnp.where(value >= size, value - size, value)

    def present(da, db):
        checks = []
        if da:
            checks.append(ax > 0 if da < 0 else ax < nx - 1)
        if db:
            checks.append(ay > 0 if db < 0 else ay < ny - 1)
        return checks[0] if len(checks) == 1 else jnp.logical_and(*checks)

    def patch(ref, da, db):
        return ref.at[pl.ds((1 + da) * rows, rows), pl.ds((1 + db) * columns, columns)]

    def halo_copy(ref, slot, index):
        da, db = SIDES[index]
        return pltpu.make_async_remote_copy(
            src_ref=patch(ref, 0, 0),
            dst_ref=patch(ref, -da, -db),
            send_sem=halo_send.at[slot, index],
            recv_sem=halo_recv.at[slot, index],
            device_id=(ax + da, ay + db),
            device_id_type=MESH,
        )

    def fold_copy(slot, index):
        da, db = SIDES[index]
        first, extent = (rows - OV if da < 0 else 0), (OV if da else rows)
        lanes = pl.ds((1 + db) * columns, columns)
        return pltpu.make_async_remote_copy(
            src_ref=total.at[slot, pl.ds((1 + da) * rows + first, extent), lanes],
            dst_ref=fold.at[slot, index, pl.ds(first, extent)],
            send_sem=fold_send.at[slot, index],
            recv_sem=fold_recv.at[slot, index],
            device_id=(ax + da, ay + db),
            device_id_type=MESH,
        )

    def start_sides(make):
        for index, (da, db) in enumerate(SIDES):

            @pl.when(present(da, db))
            def _(index=index):
                make(index).start()

    def wait_sides(make):
        for index, (da, db) in enumerate(SIDES):

            @pl.when(present(-da, -db))
            def _(index=index):
                make(index).wait_recv()

    def gather_copy(slot, tx, ty):
        return pltpu.make_async_remote_copy(
            src_ref=message.at[slot],
            dst_ref=gathered.at[slot, me],
            send_sem=gather_send.at[slot],
            recv_sem=gather_recv.at[slot],
            device_id=(tx, ty),
            device_id_type=MESH,
        )

    def scatter_copy(slot, tx, ty):
        return pltpu.make_async_remote_copy(
            src_ref=terms.at[slot, tx * ny + ty],
            dst_ref=scattered.at[slot, me],
            send_sem=scatter_send.at[slot],
            recv_sem=scatter_recv.at[slot],
            device_id=(tx, ty),
            device_id_type=MESH,
        )

    def everything(ref, send, recv, slot):
        span = ref.at[slot, pl.ds(0, count - 1)]
        return pltpu.make_async_remote_copy(
            src_ref=span,
            dst_ref=span,
            send_sem=send.at[slot],
            recv_sem=recv.at[slot],
            device_id=(wrap(ax + 1, nx), ay),
            device_id_type=MESH,
        )

    def others(act):
        columns_of = [ay] + [wrap(ay + step, ny) for step in range(1, ny)]
        def one(offset, carry):
            tx = wrap(ax + offset, nx)
            for ty in columns_of:
                act(tx, ty)
            return carry

        lax.fori_loop(1, nx, one, 0, unroll=nx - 1 if nx <= 8 else 1)
        for ty in columns_of[1:]:
            act(ax, ty)

    frames[...] = jnp.zeros_like(frames)
    cond[...] = jnp.zeros_like(cond)
    fold[...] = jnp.zeros_like(fold)
    total[...] = jnp.zeros_like(total)
    barrier = pltpu.get_barrier_semaphore()
    others(
        lambda tx, ty: pl.semaphore_signal(
            barrier, inc=1, device_id=(tx, ty), device_id_type=MESH
        )
    )
    natural[...] = jnp.zeros_like(natural)
    for load in loads[:4]:
        load.wait()
    right = right_ref[...]
    classes = class_ref[...]
    conductivity = jnp.zeros((rows, columns), jnp.float32)
    for level in range(values_ref.shape[0]):
        conductivity = jnp.where(classes == level, values_ref[level], conductivity)
    cond[own] = conductivity
    frames[(0,) + own] = right
    coarse_wide[...] = jnp.zeros_like(coarse_wide)
    narrow = coarse_rows[...].astype(jnp.float32)
    for index in range(count):
        coarse_wide[0:modes, index * LANES : index * LANES + modes] = narrow[
            :, index * modes : (index + 1) * modes
        ]
    coarse_ref[...] = coarse_wide[...].astype(jnp.bfloat16)
    pl.semaphore_wait(barrier, count - 1)

    start_sides(lambda index: halo_copy(frames.at[0], 0, index))
    start_sides(lambda index: halo_copy(cond, ITERS + 1, index))
    for load in loads[4:]:
        load.wait()
    for index in range(blocks):
        factor = factors_ref[index]
        gram[index] = lax.dot_general(
            factor, factor, TN, preferred_element_type=jnp.float32
        ).astype(jnp.bfloat16)

    frame_shape = cond.shape
    row_at = lax.broadcasted_iota(jnp.int32, frame_shape, 0) + (ax - 1) * rows
    column_at = lax.broadcasted_iota(jnp.int32, frame_shape, 1) + (ay - 1) * columns
    inside = (row_at >= 0) & (row_at < nx * rows) & (column_at >= 0) & (column_at < ny * columns)
    lane = lax.broadcasted_iota(jnp.int32, (1, LANES), 1)
    keep = jnp.where(lane < kept_ref[...], 1.0, 0.0)
    keep_modes = keep[:, :MODES]

    def lane_value(row, index):
        return jnp.sum(jnp.where(lane == index, row, 0.0), axis=1, keepdims=True)

    def whole_sum(values):
        return jnp.sum(jnp.sum(values, axis=0, keepdims=True), axis=1, keepdims=True)

    def precondition(slot, values, pairs):
        wide = frame_shape[1]
        rolled = pltpu.roll(values, wide - (columns - OV), 1)
        natural[...] = rolled[rows - OV : rows - OV + ext_rows]
        for row in range(ext_rows):
            flat[0:1, ext_columns * row : ext_columns * (row + 1)] = natural[
                row : row + 1, 0:ext_columns
            ]
        box = flat[...].astype(jnp.bfloat16)
        coarse_in = lax.dot_general(
            box, basis_ref[...], NT, preferred_element_type=jnp.float32
        )
        message[slot] = jnp.zeros((1, LANES), jnp.float32)
        message[slot, :, 0:MODES] = coarse_in * keep_modes
        others(lambda tx, ty: gather_copy(slot, tx, ty).start())
        gathered[slot, me] = message[slot]
        shares = jnp.zeros((1, LANES), jnp.float32)
        for index, (first, second) in enumerate(pairs):
            shares = jnp.where(lane == MODES + index, whole_sum(first * second), shares)
        for index in range(blocks):
            at = slice(index * block, (index + 1) * block)
            solved[0:1, at] = lax.dot_general(
                box[:, at], gram[index], NN, preferred_element_type=jnp.float32
            )
        everything(gathered, gather_send, gather_recv, slot).wait_recv()
        everyone = jnp.concatenate(
            [gathered[slot, index] for index in range(count)], axis=1
        ).astype(jnp.bfloat16)
        coarse_mid = lax.dot_general(
            everyone, coarse_ref[...], NT, preferred_element_type=jnp.float32
        )
        mid_half = (coarse_mid * keep_modes).astype(jnp.bfloat16)
        spread = lax.dot_general(
            mid_half, coarse_ref[...], NN, preferred_element_type=jnp.float32
        )
        for index in range(count):
            terms[slot, index] = spread[:, index * LANES : (index + 1) * LANES] + shares
        others(lambda tx, ty: scatter_copy(slot, tx, ty).start())
        scattered[slot, me] = terms[slot, me]
        everything(scattered, scatter_send, scatter_recv, slot).wait_recv()
        sums = jnp.sum(scattered[slot], axis=0)
        coarse_out = sums * keep
        weights = coarse_out[:, :MODES].astype(jnp.bfloat16)
        solved[...] += lax.dot_general(
            weights, basis_ref[...], NN, preferred_element_type=jnp.float32
        )
        for row in range(ext_rows):
            natural[row : row + 1, 0:ext_columns] = solved[
                0:1, ext_columns * row : ext_columns * (row + 1)
            ]
        lanes = lax.broadcasted_iota(jnp.int32, natural.shape, 1)
        clean = jnp.where(lanes < ext_columns, natural[...], 0.0)
        total[slot, rows - OV : rows - OV + ext_rows, :] = pltpu.roll(clean, columns - OV, 1)
        copies = functools.partial(fold_copy, slot)
        start_sides(copies)
        result = total[(slot,) + own]
        wait_sides(copies)
        for index in range(len(SIDES)):
            result = result + fold[slot, index]
        return result, sums

    copies = lambda index: halo_copy(frames.at[0], 0, index)
    wait_sides(copies)
    z, _ = precondition(0, frames[0], ())

    copies = lambda index: halo_copy(cond, ITERS + 1, index)
    wait_sides(copies)
    cells = cond[...]
    face_north = 0.5 * (cells + pltpu.roll(cells, 1, 0))
    face_west = 0.5 * (cells + pltpu.roll(cells, 1, 1))

    def operate(field):
        north = face_north * (field - pltpu.roll(field, 1, 0))
        west = face_west * (field - pltpu.roll(field, 1, 1))
        image = north - pltpu.roll(north, frame_shape[0] - 1, 0)
        image = image + (west - pltpu.roll(west, frame_shape[1] - 1, 1))
        return jnp.where(inside, image, 0.0)

    residual = right
    field = jnp.zeros_like(right)
    direction = image = mapped = None
    energy = curvature = None
    for step in range(1, ITERS + 1):
        frames[(step,) + own] = z
        copies = functools.partial(halo_copy, frames.at[step], step)
        start_sides(copies)
        wait_sides(copies)
        applied = operate(frames[step])
        applied_own = applied[rows : 2 * rows, columns : 2 * columns]
        pairs = [(residual, z), (z, applied_own)]
        if step > 1:
            pairs.append((z, image))
        corrected, sums = precondition(step, applied, pairs)
        fresh, plain = lane_value(sums, MODES), lane_value(sums, MODES + 1)
        if step == 1:
            direction, image, mapped, curvature = z, applied_own, corrected, plain
        else:
            ratio = fresh / energy
            cross = lane_value(sums, MODES + 2)
            curvature = plain + 2.0 * ratio * cross + ratio * ratio * curvature
            direction = z + ratio * direction
            image = applied_own + ratio * image
            mapped = corrected + ratio * mapped
        energy = fresh
        length = energy / curvature
        field = field + length * direction
        residual = residual - length * image
        z = z - length * mapped

    out[0] = field
    out[1] = residual
    out[2] = z

    for slot in range(ITERS + 1):
        everything(gathered, gather_send, gather_recv, slot).wait_send()
        everything(terms, scatter_send, scatter_recv, slot).wait_send()
    for index, (da, db) in enumerate(SIDES):

        @pl.when(present(da, db))
        def _(index=index):
            halo_copy(cond, ITERS + 1, index).wait_send()
            for slot in range(ITERS + 1):
                halo_copy(frames.at[slot], slot, index).wait_send()
                fold_copy(slot, index).wait_send()


def per_device(
    shape, right_side, class_map, class_values, kept_counts, factors, basis, coarse_factor
):
    count = shape[0] * shape[1]
    rows, columns = right_side.shape
    modes = basis.shape[2]
    blocks, block = factors.shape[2:4]
    cells = blocks * block
    flat_basis = jnp.pad(basis.reshape(modes, cells), ((0, MODES - modes), (0, 0)))
    steps = ITERS + 1
    frame = (3 * rows, 3 * columns)
    vmem = pl.BlockSpec(memory_space=pltpu.VMEM)
    hbm = pl.BlockSpec(memory_space=pltpu.HBM)
    smem = pl.BlockSpec(memory_space=pltpu.SMEM)
    f32, half = jnp.float32, jnp.bfloat16
    stacked = pl.pallas_call(
        functools.partial(kernel, shape),
        out_shape=jax.ShapeDtypeStruct((3, rows, columns), f32),
        in_specs=[hbm, hbm, smem, hbm, hbm, hbm, hbm],
        out_specs=vmem,
        scratch_shapes=[
            pltpu.VMEM((rows, columns), f32),
            pltpu.VMEM((rows, columns), jnp.int32),
            pltpu.VMEM((1, 1), jnp.int32),
            pltpu.VMEM((blocks, block, block), half),
            pltpu.VMEM((MODES, cells), half),
            pltpu.VMEM(coarse_factor.shape, half),
            pltpu.SemaphoreType.DMA((6,)),
            pltpu.VMEM((blocks, block, block), half),
            pltpu.VMEM((MODES, count * LANES), f32),
            pltpu.VMEM((MODES, count * LANES), half),
            pltpu.VMEM(frame, f32),
            pltpu.VMEM((steps,) + frame, f32),
            pltpu.VMEM((steps, len(SIDES), rows, columns), f32),
            pltpu.VMEM((steps,) + frame, f32),
            pltpu.VMEM((rows + 2 * OV, 3 * columns), f32),
            pltpu.VMEM((1, cells), f32),
            pltpu.VMEM((1, cells), f32),
            pltpu.VMEM((steps, 1, LANES), f32),
            pltpu.VMEM((steps, count, 1, LANES), f32),
            pltpu.VMEM((steps, count, 1, LANES), f32),
            pltpu.VMEM((steps, count, 1, LANES), f32),
            pltpu.SemaphoreType.DMA((steps + 1, len(SIDES))),
            pltpu.SemaphoreType.DMA((steps + 1, len(SIDES))),
            pltpu.SemaphoreType.DMA((steps, len(SIDES))),
            pltpu.SemaphoreType.DMA((steps, len(SIDES))),
            pltpu.SemaphoreType.DMA((steps,)),
            pltpu.SemaphoreType.DMA((steps,)),
            pltpu.SemaphoreType.DMA((steps,)),
            pltpu.SemaphoreType.DMA((steps,)),
        ],
        compiler_params=pltpu.CompilerParams(
            collective_id=0, has_side_effects=True, vmem_limit_bytes=60 * 2**20
        ),
    )(
        right_side,
        class_map,
        class_values,
        kept_counts,
        factors.reshape(blocks, block, block),
        flat_basis,
        coarse_factor,
    )
    return (stacked[0], stacked[1], stacked[2])


def solution(mesh):
    shape = (mesh.shape["gx"], mesh.shape["gy"])
    in_specs = (
        P("gx", "gy"),
        P("gx", "gy"),
        P(),
        P("gx", "gy"),
        P("gx", "gy", None, None, None),
        P("gx", "gy", None, None, None),
        P(("gx", "gy"), None),
    )
    out_specs = (P("gx", "gy"), P("gx", "gy"), P("gx", "gy"))

    return jax.shard_map(
        functools.partial(per_device, shape),
        mesh=mesh,
        in_specs=in_specs,
        out_specs=out_specs,
        check_vma=False,
    )
```
